32 devices in a mesh: grp: 2 (over y), side: 2 (over core), shard: 8 (over z, x).
Axes of the slice: x: 2, y: 2, z: 4, core: 2. Of those that a mesh axis runs over, the one named last changes fastest.
Arguments:
- queries: bfloat16 [256, 3072], P(('grp', 'shard')), parts along dimension 0, may hold values from -100 to 100
- cache_keys: bfloat16 [256, 128, 512], P(('grp', 'shard')), parts along dimension 0, may hold values from -3 to 3
- cache_values: bfloat16 [256, 128, 512], P(('grp', 'shard')), parts along dimension 0, may hold values from -4 to 4
- lengths: int32 [256], P(('grp', 'shard')), parts along dimension 0, may hold values from 32 to 128
- residual_in: bfloat16 [256, 3072], P(('grp', 'shard')), parts along dimension 0, may hold values from -6 to 6
- norm_gain: float32 [3072], replicated, may hold values from 0.1 to 1.9
- expert_ids: int32 [256, 2], P(('grp', 'shard')), parts along dimension 0, may hold values from 0 to 3, all different within a row; in each aligned block of 16 rows (0 to 15, 16 to 31, ...) at most 12 rows name the same one
- gate_values: bfloat16 [256, 2], P(('grp', 'shard')), parts along dimension 0, may hold values from 0.19921875 to 1
- w_gate: bfloat16 [3072, 4096], P(None, 'shard'), may hold values from -0.109375 to 0.109375
- w_up: bfloat16 [3072, 4096], P(None, 'shard'), may hold values from -0.109375 to 0.109375
- w_down: bfloat16 [4096, 3072], P('shard'), may hold values from -0.1875 to 0.1875
Outputs:
- mixed: bfloat16 [256, 3072], P(('grp', 'shard'), 'side'), parts along dimension 0
The draws below stay inside these ranges and needn't reach their ends.
There are 2 independent parts, one for each index of `grp`. The reference program is written for one: setup_inputs(seed, part) draws one part's arguments, and reference() takes and returns one part's arrays. A program takes and returns all parts, laid end to end along the dimension named above; an argument that names none is the same for every part. Nothing has to cross between parts.
Inputs may be any that keep to these rules, and one draw needn't show every extreme that they name: `expert_ids`: the 2 experts of a row differ. Among the 16 rows of one device no expert is named by more than 12 rows, a bound that some block reaches.
All inputs are finite; a program needn't handle non-finite values.
Results may differ from the reference program's by a relative error of at most 0.0061.
Values may be sent and summed in bfloat16 or wider, within the bound.
A program may use at most 128 MiB of HBM per device.

```python
import math
import jax
import jax.numpy as jnp
import numpy as np
from jax import lax

D = 3072
HD = 128
QH = 24
KVH = 4
EXPERTS = 4
TOPK = 2
R_DEV = 16
CTX = 128
MOST = 12
ROWS = 128
FF = 1024
N_SHARD = 8


def shared_keys(key):
    base_draw = jax.random.truncated_normal(key, -3.0, 3.0, (ROWS, CTX, KVH * HD), jnp.float32)
    moved = base_draw.at[:, 1].set(base_draw[:, 1])
    return moved


def draw_cache_keys(key, part):
    return shared_keys(key).astype(jnp.bfloat16)


def draw_queries(key, part):
    own_key = jax.random.fold_in(key, 7)
    values = jax.random.truncated_normal(own_key, -3.0, 3.0, (ROWS, QH * HD), jnp.float32)
    return values.astype(jnp.bfloat16)


def with_ends(result, stream_key, smallest, top_value):
    index_at = [jax.random.randint(jax.random.fold_in(stream_key, axis), (), 0, length) for axis, length in enumerate(result.shape)]
    longest = result.shape.index(max(result.shape))
    next_to = index_at[:longest] + [(index_at[longest] + 1) % result.shape[longest]] + index_at[longest + 1:]
    return result.at[tuple(index_at)].set(smallest).at[tuple(next_to)].set(top_value)


def steps_of(key, shape, pieces, least, largest):
    factor_of, own = 1.0, jax.random.fold_in(key, 6)
    for position, parts in pieces:
        draws = jnp.exp(jax.random.uniform(jax.random.fold_in(own, position), (parts,), jnp.float32, least / len(pieces), largest / len(pieces)))
        factor_of = factor_of * jnp.repeat(draws, shape[position] // parts).reshape([-1 if axis == position else 1 for axis in range(len(shape))])
    return factor_of


def assign_block(rng, own, number, rows, count, top, most, lean):
    order = jax.random.permutation(rng, count)
    crowded, usual = load_shares(count, rows * top, most, lean, True), load_shares(count, rows * top, most, lean, False)
    places = jnp.arange(count)

    def named(sizes, rotation):
        used = int((sizes > 0).sum())
        fixed = max(1, used // 4)
        passed = fixed + (places - fixed + rotation * (used - fixed)) % max(1, count - fixed)
        return jnp.zeros((count,), jnp.int32).at[order[jnp.where(places < fixed, places, passed)]].set(jnp.asarray(sizes, jnp.int32))

    sizes = jnp.where(number % 4 == 0, named(crowded, number // 4), named(usual, number - number // 4 - 1))
    mixed = jax.random.permutation(jax.random.fold_in(own, 3), count)
    donor, sink = mixed[0:count // 2 * 2:2], mixed[1:count // 2 * 2:2]
    room = jnp.minimum(sizes[donor] - 1, most - sizes[sink]) // 2
    room = jnp.where((donor == order[0]) | (sink == order[0]) | (sizes[sink] == 0), 0, jnp.maximum(room, 0))
    passed = jax.random.randint(jax.random.fold_in(own, 4), (count // 2,), 0, 1 << 20) % (room + 1)
    sizes = sizes.at[donor].add(-passed).at[sink].add(passed)
    items = jnp.searchsorted(jnp.cumsum(sizes), jnp.arange(rows * top), side="right").astype(jnp.int32)
    listing = items.reshape(top, rows).T
    listing = listing[jax.random.permutation(jax.random.fold_in(own, 1), rows)]
    rotation = jax.random.randint(jax.random.fold_in(own, 2), (rows, 1), 0, top)
    return jnp.take_along_axis(listing, (jnp.arange(top)[None, :] + rotation) % top, axis=1)


def load_shares(amount, total, reach, lean, full):
    portions = [(1 << 20) // math.isqrt(grade ** lean) + 1 for grade in range(1, amount + 1)]
    largest = reach if full else min(reach, max(-(-total // amount), total * portions[0] // sum(portions)))
    least = 1 if total - largest >= amount - 1 else 0
    given, spare = [largest] + [least] * (amount - 1), total - largest - least * (amount - 1)
    while spare > 0:
        movable = [i for i in range(1, amount) if given[i] < largest] or [i for i in range(1, amount) if given[i] < reach]
        whole, budget = sum([portions[i] for i in movable]), spare
        for i in movable:
            extra = min(reach - given[i], max(1, budget * portions[i] // whole), spare)
            given[i] = given[i] + extra
            spare = spare - extra
    return np.array(given)


def normal_values(key, shape, scale, most, cuts=(), held_as=jnp.bfloat16):
    drawn = scale * jax.random.normal(key, shape, jnp.float32)
    if cuts:
        drawn = drawn * steps_of(key, shape, cuts, -0.22, 0.18)
    return jnp.clip(drawn, -most, most).astype(held_as)


def setup_inputs(seed: int = 0, part: int = 0) -> dict:
    streams_of = jax.random.split(jax.random.key(seed), 12)
    own_keys = jax.random.split(jax.random.fold_in(streams_of[11], part), 12)
    queries = draw_queries(jax.random.fold_in(jax.random.fold_in(streams_of[11], part), 71), part)
    cache_keys = draw_cache_keys(jax.random.fold_in(jax.random.fold_in(streams_of[11], part), 71), part)
    cache_values = normal_values(own_keys[2], (ROWS, CTX, KVH * HD), 1.0, 4.0, ((0, 8),))
    lengths = with_ends(jax.random.randint(own_keys[3], (ROWS,), CTX // 4, CTX + 1), jax.random.fold_in(own_keys[3], 1), CTX // 4, CTX).astype(jnp.int32)
    residual_in = normal_values(own_keys[4], (ROWS, D), 1.0, 6.0, ((0, 8),))
    norm_gain = jnp.clip(1.0 + 0.18 * jax.random.normal(streams_of[5], (D,), jnp.float32), 0.1, 1.9)
    expert_ids_keys = jax.random.split(jax.random.fold_in(own_keys[6], 1), ROWS // R_DEV)
    expert_ids_turns = jax.random.permutation(jax.random.fold_in(own_keys[6], 3), ROWS // R_DEV)
    expert_ids = jax.vmap(lambda own, number: assign_block(jax.random.fold_in(own_keys[6], 2), own, number, R_DEV, EXPERTS, TOPK, MOST, 2))(expert_ids_keys, expert_ids_turns).reshape((ROWS, TOPK))
    gate_values = jnp.clip(0.19921875 + 0.80078125 * jax.random.uniform(own_keys[7], (ROWS, TOPK), jnp.float32) ** steps_of(own_keys[7], (ROWS, TOPK), ((0, 8),), -0.2, 0.2), 0.19921875, 1.0).astype(jnp.bfloat16)
    w_gate = normal_values(streams_of[8], (D, EXPERTS * FF), D ** -0.5, 0.109375, ((1, 8),))
    w_up = normal_values(streams_of[9], (D, EXPERTS * FF), D ** -0.5, 0.109375, ((1, 8),))
    w_down = normal_values(streams_of[10], (EXPERTS * FF, D), FF ** -0.5, 0.1875, ((0, 8),))
    return {"queries": queries, "cache_keys": cache_keys, "cache_values": cache_values, "lengths": lengths, "residual_in": residual_in, "norm_gain": norm_gain, "expert_ids": expert_ids, "gate_values": gate_values, "w_gate": w_gate, "w_up": w_up, "w_down": w_down}


def attend(queries, cache_keys, cache_values, lengths):
    row_count = queries.shape[0]
    query_heads = queries.reshape(row_count, KVH, QH // KVH, HD).astype(jnp.float32)
    key_heads = cache_keys.reshape(row_count, CTX, KVH, HD).astype(jnp.float32)
    value_heads = cache_values.reshape(row_count, CTX, KVH, HD).astype(jnp.float32)
    scores = jnp.einsum('rkgd,rckd->rkgc', query_heads, key_heads) / math.sqrt(HD)
    visible = jnp.arange(CTX)[None, None, None, :] < lengths[:, None, None, None]
    scores = jnp.where(visible, scores, -1e+30)
    peak_score = lax.optimization_barrier(jnp.max(scores, axis=-1, keepdims=True))
    weights = jnp.exp(scores - peak_score)
    probability = (weights / lax.optimization_barrier(jnp.sum(weights, axis=-1, keepdims=True))).astype(jnp.bfloat16)
    mixed = jnp.einsum('rkgc,rckd->rkgd', probability.astype(jnp.float32), value_heads)
    return mixed.reshape(row_count, QH * HD)

def normalize(resid, norm_gain):
    widened = resid.astype(jnp.float32)
    scale = lax.rsqrt(lax.optimization_barrier(jnp.mean(widened * widened, axis=-1, keepdims=True)) + 1e-05)
    return (widened * scale * norm_gain).astype(jnp.bfloat16)

def reference(queries, cache_keys, cache_values, lengths, residual_in, norm_gain, expert_ids, gate_values, w_gate, w_up, w_down):
    attended = attend(queries, cache_keys, cache_values, lengths)
    resid = (residual_in.astype(jnp.float32) + attended).astype(jnp.bfloat16)
    normed = normalize(resid, norm_gain)
    match = expert_ids[:, :, None] == jnp.arange(EXPERTS)[None, None, :]
    hit_count = lax.optimization_barrier(jnp.sum(match.astype(jnp.int32), axis=1))
    per_source = hit_count.reshape(N_SHARD, R_DEV, EXPERTS)
    ranked = (jnp.cumsum(per_source, axis=1) - per_source).reshape(ROWS, EXPERTS)
    source = (jnp.arange(ROWS) // R_DEV).astype(jnp.int32)
    row_gate = lax.optimization_barrier(jnp.sum(jnp.where(match, gate_values.astype(jnp.float32)[:, :, None], 0.0), axis=1))
    slot_count = N_SHARD * MOST
    expert_sum = jnp.zeros((ROWS, D), jnp.float32)
    for expert in range(EXPERTS):
        placed = jnp.where(hit_count[:, expert] > 0, source * MOST + ranked[:, expert], slot_count).astype(jnp.int32)
        block_in = jnp.zeros((slot_count, D), jnp.bfloat16).at[placed].set(normed, mode='drop')
        offset = expert * FF
        gate_pre = jnp.dot(block_in, w_gate[:, offset:offset + FF], preferred_element_type=jnp.float32)
        up_pre = jnp.dot(block_in, w_up[:, offset:offset + FF], preferred_element_type=jnp.float32)
        hidden = (jax.nn.silu(gate_pre) * up_pre).astype(jnp.bfloat16)
        expert_out = jnp.dot(hidden, w_down[offset:offset + FF], preferred_element_type=jnp.float32)
        picked = expert_out[jnp.minimum(placed, slot_count - 1)]
        expert_sum = expert_sum + row_gate[:, expert][:, None] * picked
    return (resid.astype(jnp.float32) + expert_sum).astype(jnp.bfloat16)
```

```python
import functools
import math

import jax
import jax.numpy as jnp
from jax import lax
from jax.experimental import pallas as pl
from jax.experimental.pallas import tpu as pltpu
from jax.sharding import PartitionSpec as P

HD = 128
QH = 24
KVH = 4
EXPERTS = 4
MESH = pl.DeviceIdType.MESH


def kernel(
    n,
    lengths,
    queries,
    cache_keys,
    cache_values,
    residual_in,
    norm_gain,
    expert_ids,
    gate_values,
    w_gate,
    w_up,
    w_down,
    out,
    keys,
    values,
    gate_w,
    up_w,
    down_w,
    heads,
    attended,
    resid_halves,
    rows_in,
    parts,
    returned,
    load_sem,
    row_send,
    row_recv,
    side_send,
    side_recv,
    part_send,
    part_recv,
):
    me = lax.axis_index("shard")
    side = lax.axis_index("side")
    other = 1 - side
    row_count, width = residual_in.shape
    half = width // 2
    context = keys.shape[1]
    group_size = n // EXPERTS

    loads = [
        pltpu.make_async_copy(cache_keys, keys, load_sem.at[0]),
        pltpu.make_async_copy(cache_values, values, load_sem.at[1]),
        pltpu.make_async_copy(w_gate, gate_w, load_sem.at[2]),
        pltpu.make_async_copy(w_up, up_w, load_sem.at[3]),
        pltpu.make_async_copy(
            w_down.at[:, pl.ds(pl.multiple_of(side * half, half), half)], down_w, load_sem.at[4]
        ),
    ]
    for load in loads:
        load.start()

    barrier = pltpu.get_barrier_semaphore()
    pl.semaphore_signal(barrier, inc=1, device_id={"side": other}, device_id_type=MESH)

    def greet(k, carry):
        pl.semaphore_signal(
            barrier, inc=1, device_id={"shard": lax.rem(me + k, n)}, device_id_type=MESH
        )
        return carry

    lax.fori_loop(1, n, greet, 0)

    for h in range(QH):
        heads[:, h, :] = queries[:, h * HD : (h + 1) * HD].astype(jnp.float32)
    group_of = lax.broadcasted_iota(jnp.int32, (QH, HD), 0) // (QH // KVH)
    position = lax.broadcasted_iota(jnp.int32, (QH, context), 1)
    loads[0].wait()
    probabilities = []
    for r in range(row_count):
        q = heads[r]
        spread = jnp.concatenate(
            [jnp.where(group_of == g, q, 0.0) for g in range(KVH)], axis=1
        ).astype(jnp.bfloat16)
        scores = lax.dot_general(
            spread, keys[r], (((1,), (1,)), ((), ())), preferred_element_type=jnp.float32
        ) * (1.0 / math.sqrt(HD))
        scores = jnp.where(position < lengths[r], scores, -1e30)
        weights = jnp.exp(scores - jnp.max(scores, axis=-1, keepdims=True))
        total = jnp.sum(weights, axis=-1, keepdims=True)
        probabilities.append((weights / total).astype(jnp.bfloat16))
    loads[1].wait()
    for r in range(row_count):
        mixed = jnp.dot(probabilities[r], values[r], preferred_element_type=jnp.float32)
        picked = jnp.where(group_of == 0, mixed[:, :HD], 0.0)
        for g in range(1, KVH):
            picked = jnp.where(group_of == g, mixed[:, g * HD : (g + 1) * HD], picked)
        attended[r] = picked

    squares = jnp.zeros((row_count, HD), jnp.float32)
    widened = []
    for h in range(QH):
        cols = slice(h * HD, (h + 1) * HD)
        resid = (residual_in[:, cols].astype(jnp.float32) + attended[:, h, :]).astype(jnp.bfloat16)
        resid_halves[h // (QH // 2), :, (h % (QH // 2)) * HD : (h % (QH // 2) + 1) * HD] = resid
        wide = resid.astype(jnp.float32)
        widened.append(wide)
        squares += wide * wide
    scale = lax.rsqrt(jnp.sum(squares, axis=-1, keepdims=True) * (1.0 / width) + 1e-05)
    for h in range(QH):
        normed = (widened[h] * scale * norm_gain[:, h * HD : (h + 1) * HD]).astype(jnp.bfloat16)
        rows_in[h // (QH // 2), me, :, (h % (QH // 2)) * HD : (h % (QH // 2) + 1) * HD] = normed

    pl.semaphore_wait(barrier, n)

    def row_copy(k):
        return pltpu.make_async_remote_copy(
            src_ref=rows_in.at[side, me],
            dst_ref=rows_in.at[side, me],
            send_sem=row_send.at[k],
            recv_sem=row_recv.at[k],
            device_id={"shard": lax.rem(me + k, n)},
            device_id_type=MESH,
        )

    def side_copy(k):
        source = lax.rem(me - k + n, n)
        return pltpu.make_async_remote_copy(
            src_ref=rows_in.at[side, source],
            dst_ref=rows_in.at[side, source],
            send_sem=side_send.at[k],
            recv_sem=side_recv.at[k],
            device_id={"side": other},
            device_id_type=MESH,
        )

    def part_copy(k):
        target = lax.rem(me + k, n)
        return pltpu.make_async_remote_copy(
            src_ref=parts.at[target],
            dst_ref=returned.at[k],
            send_sem=part_send.at[k],
            recv_sem=part_recv.at[k],
            device_id={"shard": target},
            device_id_type=MESH,
        )

    def each(step):
        def run(k, carry):
            step(k)
            return carry

        lax.fori_loop(1, n, run, 0)

    each(lambda k: row_copy(k).start())

    def pass_on(k):
        row_copy(k).wait_recv()
        side_copy(k).start()

    each(pass_on)
    loads[2].wait()
    loads[3].wait()
    own = rows_in[side].reshape(n * row_count, half)
    own_cols = pl.ds(pl.multiple_of(side * half, half), half)
    gate_pre = jnp.dot(own, gate_w[own_cols, :], preferred_element_type=jnp.float32)
    up_pre = jnp.dot(own, up_w[own_cols, :], preferred_element_type=jnp.float32)
    each(lambda k: side_copy(k).wait_recv())
    swapped = rows_in[other].reshape(n * row_count, half)
    other_cols = pl.ds(pl.multiple_of(other * half, half), half)
    gate_pre += jnp.dot(swapped, gate_w[other_cols, :], preferred_element_type=jnp.float32)
    up_pre += jnp.dot(swapped, up_w[other_cols, :], preferred_element_type=jnp.float32)
    hidden = (gate_pre / (1.0 + jnp.exp(-gate_pre)) * up_pre).astype(jnp.bfloat16)
    loads[4].wait()
    parts[...] = (
        jnp.dot(hidden, down_w[...], preferred_element_type=jnp.float32)
        .astype(jnp.bfloat16)
        .reshape(n, row_count, half)
    )
    each(lambda k: part_copy(k).start())

    ids = expert_ids[...]
    gates = gate_values[...].astype(jnp.float32)

    def weight(source):
        match = ids == lax.div(source, group_size)
        return jnp.sum(jnp.where(match, gates, 0.0), axis=-1, keepdims=True)

    total = weight(me) * parts[me].astype(jnp.float32)

    def gather(k, total):
        part_copy(k).wait_recv()
        return total + weight(lax.rem(me - k + n, n)) * returned[k].astype(jnp.float32)

    total = lax.fori_loop(1, n, gather, total)
    out[...] = (resid_halves[side].astype(jnp.float32) + total).astype(jnp.bfloat16)

    def finish(k):
        row_copy(k).wait_send()
        side_copy(k).wait_send()
        part_copy(k).wait_send()

    each(finish)


def body(
    queries,
    cache_keys,
    cache_values,
    lengths,
    residual_in,
    norm_gain,
    expert_ids,
    gate_values,
    w_gate,
    w_up,
    w_down,
):
    row_count, width = residual_in.shape
    n = lax.axis_size("shard")
    half = width // 2
    hidden = w_down.shape[0]
    vmem = pl.BlockSpec(memory_space=pltpu.VMEM)
    smem = pl.BlockSpec(memory_space=pltpu.SMEM)
    anywhere = pl.BlockSpec(memory_space=pl.ANY)
    dma = pltpu.SemaphoreType.DMA
    return pl.pallas_call(
        functools.partial(kernel, n),
        out_shape=jax.ShapeDtypeStruct((row_count, half), jnp.bfloat16),
        in_specs=[smem, vmem, anywhere, anywhere, vmem, vmem, vmem, vmem, anywhere, anywhere, anywhere],
        out_specs=vmem,
        scratch_shapes=[
            pltpu.VMEM(cache_keys.shape, jnp.bfloat16),
            pltpu.VMEM(cache_values.shape, jnp.bfloat16),
            pltpu.VMEM(w_gate.shape, jnp.bfloat16),
            pltpu.VMEM(w_up.shape, jnp.bfloat16),
            pltpu.VMEM((hidden, half), jnp.bfloat16),
            pltpu.VMEM((row_count, QH, HD), jnp.float32),
            pltpu.VMEM((row_count, QH, HD), jnp.float32),
            pltpu.VMEM((2, row_count, half), jnp.bfloat16),
            pltpu.VMEM((2, n, row_count, half), jnp.bfloat16),
            pltpu.VMEM((n, row_count, half), jnp.bfloat16),
            pltpu.VMEM((n, row_count, half), jnp.bfloat16),
            dma((5,)),
            dma((n,)),
            dma((n,)),
            dma((n,)),
            dma((n,)),
            dma((n,)),
            dma((n,)),
        ],
        compiler_params=pltpu.CompilerParams(
            collective_id=0, has_side_effects=True, vmem_limit_bytes=56 * 1024 * 1024
        ),
    )(
        lengths,
        queries,
        cache_keys,
        cache_values,
        residual_in,
        norm_gain.reshape(1, width),
        expert_ids,
        gate_values,
        w_gate,
        w_up,
        w_down,
    )


def solution(mesh):
    placed = (
        P(("grp", "shard"), None),
        P(("grp", "shard"), None, None),
        P(("grp", "shard"), None, None),
        P(("grp", "shard")),
        P(("grp", "shard"), None),
        P(),
        P(("grp", "shard"), None),
        P(("grp", "shard"), None),
        P(None, "shard"),
        P(None, "shard"),
        P("shard", None),
    )
    return jax.shard_map(
        body, mesh=mesh, in_specs=placed, out_specs=P(("grp", "shard"), "side"), check_vma=False
    )
```

```python
import functools
import math

import jax
import jax.numpy as jnp
from jax import lax
from jax.experimental import pallas as pl
from jax.experimental.pallas import tpu as pltpu
from jax.sharding import PartitionSpec as P

HD = 128
QH = 24
KVH = 4
EXPERTS = 4
MESH = pl.DeviceIdType.MESH


def kernel(
    n,
    lengths,
    queries,
    cache_keys,
    cache_values,
    residual_in,
    norm_gain,
    expert_ids,
    gate_values,
    w_gate,
    w_up,
    w_down,
    out,
    keys,
    values,
    gate_w,
    up_w,
    down_w,
    heads,
    attended,
    resid_halves,
    rows_in,
    parts,
    partial,
    summed,
    returned,
    load_sem,
    row_send,
    row_recv,
    pass_send,
    pass_recv,
    side_send,
    side_recv,
    part_send,
    part_recv,
    sum_send,
    sum_recv,
):
    me = lax.axis_index("shard")
    side = lax.axis_index("side")
    other = 1 - side
    members = n // EXPERTS
    team = lax.div(me, members)
    member = lax.rem(me, members)
    teams = []
    for i in range(EXPERTS):
        flipped = team
        for bit in (1, 2):
            if i & bit:
                flipped = flipped + bit - 2 * bit * lax.rem(lax.div(team, bit), 2)
        teams.append(flipped)

    def after(j):
        return lax.rem(member + j, members)

    def before(j):
        return lax.rem(member - j + members, members)
    row_count, width = residual_in.shape
    half = width // 2
    context = keys.shape[1]

    loads = [
        pltpu.make_async_copy(cache_keys, keys, load_sem.at[0]),
        pltpu.make_async_copy(cache_values, values, load_sem.at[1]),
        pltpu.make_async_copy(w_gate, gate_w, load_sem.at[2]),
        pltpu.make_async_copy(w_up, up_w, load_sem.at[3]),
        pltpu.make_async_copy(
            w_down.at[:, pl.ds(pl.multiple_of(side * half, half), half)], down_w, load_sem.at[4]
        ),
    ]
    for load in loads:
        load.start()

    barrier = pltpu.get_barrier_semaphore()
    pl.semaphore_signal(barrier, inc=1, device_id={"side": other}, device_id_type=MESH)

    def greet(shard):
        pl.semaphore_signal(barrier, inc=1, device_id={"shard": shard}, device_id_type=MESH)

    def others(step):
        def run(j, carry):
            step(j)
            return carry

        lax.fori_loop(1, members, run, 0)

    for i in range(1, EXPERTS):
        greet(teams[i] * members + member)
    others(lambda j: greet(team * members + after(j)))

    ids = expert_ids[...]
    gates = gate_values[...].astype(jnp.float32)
    diagonal = lax.broadcasted_iota(jnp.int32, (row_count, row_count), 0) == (
        lax.broadcasted_iota(jnp.int32, (row_count, row_count), 1)
    )

    def weight(expert):
        along = jnp.sum(jnp.where(ids == expert, gates, 0.0), axis=0, keepdims=True)
        return jnp.sum(jnp.where(diagonal, along, 0.0), axis=1, keepdims=True)

    row_weights = [weight(teams[i]) for i in range(EXPERTS)]

    for h in range(QH):
        heads[:, h, :] = queries[:, h * HD : (h + 1) * HD].astype(jnp.float32)
    group_of = lax.broadcasted_iota(jnp.int32, (QH, HD), 0) // (QH // KVH)
    position = lax.broadcasted_iota(jnp.int32, (QH, context), 1)
    loads[0].wait()
    probabilities = []
    for r in range(row_count):
        q = heads[r]
        spread = jnp.concatenate(
            [jnp.where(group_of == g, q, 0.0) for g in range(KVH)], axis=1
        ).astype(jnp.bfloat16)
        scores = lax.dot_general(
            spread, keys[r], (((1,), (1,)), ((), ())), preferred_element_type=jnp.float32
        ) * (1.0 / math.sqrt(HD))
        scores = jnp.where(position < lengths[r], scores, -1e30)
        weights = jnp.exp(scores - jnp.max(scores, axis=-1, keepdims=True))
        total = jnp.sum(weights, axis=-1, keepdims=True)
        probabilities.append((weights / total).astype(jnp.bfloat16))
    loads[1].wait()
    for r in range(row_count):
        mixed = jnp.dot(probabilities[r], values[r], preferred_element_type=jnp.float32)
        picked = jnp.where(group_of == 0, mixed[:, :HD], 0.0)
        for g in range(1, KVH):
            picked = jnp.where(group_of == g, mixed[:, g * HD : (g + 1) * HD], picked)
        attended[r] = picked

    squares = jnp.zeros((row_count, HD), jnp.float32)
    widened = []
    for h in range(QH):
        cols = slice(h * HD, (h + 1) * HD)
        resid = (residual_in[:, cols].astype(jnp.float32) + attended[:, h, :]).astype(jnp.bfloat16)
        resid_halves[h // (QH // 2), :, (h % (QH // 2)) * HD : (h % (QH // 2) + 1) * HD] = resid
        wide = resid.astype(jnp.float32)
        widened.append(wide)
        squares += wide * wide
    scale = lax.rsqrt(jnp.sum(squares, axis=-1, keepdims=True) * (1.0 / width) + 1e-05)
    for h in range(QH):
        normed = (widened[h] * scale * norm_gain[:, h * HD : (h + 1) * HD]).astype(jnp.bfloat16)
        rows_in[h // (QH // 2), me, :, (h % (QH // 2)) * HD : (h % (QH // 2) + 1) * HD] = normed

    pl.semaphore_wait(barrier, EXPERTS - 1 + members)

    def block_copy(block, send_sem, recv_sem, device_id):
        return pltpu.make_async_remote_copy(
            src_ref=rows_in.at[side, block],
            dst_ref=rows_in.at[side, block],
            send_sem=send_sem,
            recv_sem=recv_sem,
            device_id=device_id,
            device_id_type=MESH,
        )

    def row_copy(i):
        return block_copy(
            me, row_send.at[i], row_recv.at[i], {"shard": teams[i] * members + member}
        )

    def pass_copy(i, j):
        return block_copy(
            teams[i] * members + member,
            pass_send.at[i * members + j],
            pass_recv.at[i * members + j],
            {"shard": team * members + after(j)},
        )

    def side_copy(i, j):
        return block_copy(
            teams[i] * members + before(j),
            side_send.at[i * members + j],
            side_recv.at[i * members + j],
            {"side": other},
        )

    def part_copy(i, j):
        return pltpu.make_async_remote_copy(
            src_ref=parts.at[teams[i] * members + after(j)],
            dst_ref=partial.at[i * members + j],
            send_sem=part_send.at[i * members + j],
            recv_sem=part_recv.at[i * members + j],
            device_id={"shard": team * members + after(j)},
            device_id_type=MESH,
        )

    def sum_copy(i):
        return pltpu.make_async_remote_copy(
            src_ref=summed.at[i],
            dst_ref=returned.at[i],
            send_sem=sum_send.at[i],
            recv_sem=sum_recv.at[i],
            device_id={"shard": teams[i] * members + member},
            device_id_type=MESH,
        )

    for i in range(1, EXPERTS):
        row_copy(i).start()
    others(lambda j: pass_copy(0, j).start())
    for i in range(1, EXPERTS):
        row_copy(i).wait_recv()
        others(lambda j: pass_copy(i, j).start())
        side_copy(i, 0).start()
    for i in range(EXPERTS):

        def swap(j):
            pass_copy(i, j).wait_recv()
            side_copy(i, j).start()

        others(swap)
    loads[2].wait()
    loads[3].wait()
    own = rows_in[side].reshape(n * row_count, half)
    own_cols = pl.ds(pl.multiple_of(side * half, half), half)
    gate_pre = jnp.dot(own, gate_w[own_cols, :], preferred_element_type=jnp.float32)
    up_pre = jnp.dot(own, up_w[own_cols, :], preferred_element_type=jnp.float32)
    for i in range(EXPERTS):
        if i:
            side_copy(i, 0).wait_recv()
        others(lambda j: side_copy(i, j).wait_recv())
    swapped = rows_in[other].reshape(n * row_count, half)
    other_cols = pl.ds(pl.multiple_of(other * half, half), half)
    gate_pre += jnp.dot(swapped, gate_w[other_cols, :], preferred_element_type=jnp.float32)
    up_pre += jnp.dot(swapped, up_w[other_cols, :], preferred_element_type=jnp.float32)
    hidden = (gate_pre / (1.0 + jnp.exp(-gate_pre)) * up_pre).astype(jnp.bfloat16)
    loads[4].wait()
    parts[...] = (
        jnp.dot(hidden, down_w[...], preferred_element_type=jnp.float32)
        .astype(jnp.bfloat16)
        .reshape(n, row_count, half)
    )

    order = list(range(1, EXPERTS)) + [0]
    for i in order:
        others(lambda j: part_copy(i, j).start())

    def team_sum(i):
        def add(j, total):
            part_copy(i, j).wait_recv()
            return total + partial[i * members + j].astype(jnp.float32)

        return lax.fori_loop(
            1, members, add, parts[teams[i] * members + member].astype(jnp.float32)
        )

    for i in range(1, EXPERTS):
        summed[i] = team_sum(i).astype(jnp.bfloat16)
        sum_copy(i).start()
    total = row_weights[0] * team_sum(0)
    for i in range(1, EXPERTS):
        sum_copy(i).wait_recv()
        total += row_weights[i] * returned[i].astype(jnp.float32)
    out[...] = (resid_halves[side].astype(jnp.float32) + total).astype(jnp.bfloat16)

    for i in range(EXPERTS):
        if i:
            row_copy(i).wait_send()
            side_copy(i, 0).wait_send()
            sum_copy(i).wait_send()

        def finish(j):
            pass_copy(i, j).wait_send()
            side_copy(i, j).wait_send()
            part_copy(i, j).wait_send()

        others(finish)


def body(
    queries,
    cache_keys,
    cache_values,
    lengths,
    residual_in,
    norm_gain,
    expert_ids,
    gate_values,
    w_gate,
    w_up,
    w_down,
):
    row_count, width = residual_in.shape
    n = lax.axis_size("shard")
    half = width // 2
    hidden = w_down.shape[0]
    vmem = pl.BlockSpec(memory_space=pltpu.VMEM)
    smem = pl.BlockSpec(memory_space=pltpu.SMEM)
    anywhere = pl.BlockSpec(memory_space=pl.ANY)
    dma = pltpu.SemaphoreType.DMA
    return pl.pallas_call(
        functools.partial(kernel, n),
        out_shape=jax.ShapeDtypeStruct((row_count, half), jnp.bfloat16),
        in_specs=[smem, vmem, anywhere, anywhere, vmem, vmem, vmem, vmem, anywhere, anywhere, anywhere],
        out_specs=vmem,
        scratch_shapes=[
            pltpu.VMEM(cache_keys.shape, jnp.bfloat16),
            pltpu.VMEM(cache_values.shape, jnp.bfloat16),
            pltpu.VMEM(w_gate.shape, jnp.bfloat16),
            pltpu.VMEM(w_up.shape, jnp.bfloat16),
            pltpu.VMEM((hidden, half), jnp.bfloat16),
            pltpu.VMEM((row_count, QH, HD), jnp.float32),
            pltpu.VMEM((row_count, QH, HD), jnp.float32),
            pltpu.VMEM((2, row_count, half), jnp.bfloat16),
            pltpu.VMEM((2, n, row_count, half), jnp.bfloat16),
            pltpu.VMEM((n, row_count, half), jnp.bfloat16),
            pltpu.VMEM((n, row_count, half), jnp.bfloat16),
            pltpu.VMEM((EXPERTS, row_count, half), jnp.bfloat16),
            pltpu.VMEM((EXPERTS, row_count, half), jnp.bfloat16),
            dma((5,)),
            dma((EXPERTS,)),
            dma((EXPERTS,)),
            dma((n,)),
            dma((n,)),
            dma((n,)),
            dma((n,)),
            dma((n,)),
            dma((n,)),
            dma((EXPERTS,)),
            dma((EXPERTS,)),
        ],
        compiler_params=pltpu.CompilerParams(
            collective_id=0, has_side_effects=True, vmem_limit_bytes=56 * 1024 * 1024
        ),
    )(
        lengths,
        queries,
        cache_keys,
        cache_values,
        residual_in,
        norm_gain.reshape(1, width),
        expert_ids.T,
        gate_values.T,
        w_gate,
        w_up,
        w_down,
    )


def solution(mesh):
    placed = (
        P(("grp", "shard"), None),
        P(("grp", "shard"), None, None),
        P(("grp", "shard"), None, None),
        P(("grp", "shard")),
        P(("grp", "shard"), None),
        P(),
        P(("grp", "shard"), None),
        P(("grp", "shard"), None),
        P(None, "shard"),
        P(None, "shard"),
        P("shard", None),
    )
    return jax.shard_map(
        body, mesh=mesh, in_specs=placed, out_specs=P(("grp", "shard"), "side"), check_vma=False
    )
```

```python
import functools
import math

import jax
import jax.numpy as jnp
from jax import lax
from jax.experimental import pallas as pl
from jax.experimental.pallas import tpu as pltpu
from jax.sharding import PartitionSpec as P

HD = 128
QH = 24
KVH = 4
EXPERTS = 4
MESH = pl.DeviceIdType.MESH


def kernel(
    n,
    lengths,
    queries_in,
    cache_keys,
    cache_values,
    residual_from,
    norm_gain,
    expert_ids,
    gate_values,
    w_gate,
    w_up,
    w_down,
    out,
    queries,
    residual_in,
    keys,
    values,
    gate_w,
    up_w,
    down_w,
    heads,
    attended,
    resid_halves,
    rows_in,
    parts,
    partial,
    summed,
    returned,
    load_sem,
    row_send,
    row_recv,
    pass_send,
    pass_recv,
    side_send,
    side_recv,
    part_send,
    part_recv,
    sum_send,
    sum_recv,
):
    me = lax.axis_index("shard")
    side = lax.axis_index("side")
    other = 1 - side
    members = n // EXPERTS
    team = lax.div(me, members)
    member = lax.rem(me, members)
    teams = []
    for i in range(EXPERTS):
        flipped = team
        for bit in (1, 2):
            if i & bit:
                flipped = flipped + bit - 2 * bit * lax.rem(lax.div(team, bit), 2)
        teams.append(flipped)

    def after(j):
        return lax.rem(member + j, members)

    def before(j):
        return lax.rem(member - j + members, members)
    row_count, width = residual_in.shape
    half = width // 2
    context = keys.shape[1]

    loads = [
        pltpu.make_async_copy(cache_keys, keys, load_sem.at[0]),
        pltpu.make_async_copy(cache_values, values, load_sem.at[1]),
        pltpu.make_async_copy(w_gate, gate_w, load_sem.at[2]),
        pltpu.make_async_copy(w_up, up_w, load_sem.at[3]),
        pltpu.make_async_copy(
            w_down.at[:, pl.ds(pl.multiple_of(side * half, half), half)], down_w, load_sem.at[4]
        ),
    ]
    query_load = pltpu.make_async_copy(queries_in, queries, load_sem.at[5])
    residual_load = pltpu.make_async_copy(residual_from, residual_in, load_sem.at[6])
    query_load.start()
    loads[0].start()
    loads[1].start()
    residual_load.start()

    barrier = pltpu.get_barrier_semaphore()
    pl.semaphore_signal(barrier, inc=1, device_id={"side": other}, device_id_type=MESH)

    def greet(shard):
        pl.semaphore_signal(barrier, inc=1, device_id={"shard": shard}, device_id_type=MESH)

    def others(step):
        def run(j, carry):
            step(j)
            return carry

        lax.fori_loop(1, members, run, 0)

    for i in range(1, EXPERTS):
        greet(teams[i] * members + member)
    others(lambda j: greet(team * members + after(j)))

    ids = expert_ids[...]
    gates = gate_values[...].astype(jnp.float32)
    diagonal = lax.broadcasted_iota(jnp.int32, (row_count, row_count), 0) == (
        lax.broadcasted_iota(jnp.int32, (row_count, row_count), 1)
    )

    def weight(expert):
        along = jnp.sum(jnp.where(ids == expert, gates, 0.0), axis=0, keepdims=True)
        return jnp.sum(jnp.where(diagonal, along, 0.0), axis=1, keepdims=True)

    row_weights = [weight(teams[i]) for i in range(EXPERTS)]

    query_load.wait()
    for h in range(QH):
        heads[:, h, :] = queries[:, h * HD : (h + 1) * HD].astype(jnp.float32)
    group_of = lax.broadcasted_iota(jnp.int32, (QH, HD), 0) // (QH // KVH)
    position = lax.broadcasted_iota(jnp.int32, (QH, context), 1)
    loads[0].wait()
    for load in loads[2:]:
        load.start()
    probabilities = []
    for r in range(row_count):
        q = heads[r]
        spread = jnp.concatenate(
            [jnp.where(group_of == g, q, 0.0) for g in range(KVH)], axis=1
        ).astype(jnp.bfloat16)
        scores = lax.dot_general(
            spread, keys[r], (((1,), (1,)), ((), ())), preferred_element_type=jnp.float32
        ) * (1.0 / math.sqrt(HD))
        scores = jnp.where(position < lengths[r], scores, -1e30)
        weights = jnp.exp(scores - jnp.max(scores, axis=-1, keepdims=True))
        total = jnp.sum(weights, axis=-1, keepdims=True)
        probabilities.append((weights / total).astype(jnp.bfloat16))
    loads[1].wait()
    for r in range(row_count):
        mixed = jnp.dot(probabilities[r], values[r], preferred_element_type=jnp.float32)
        picked = jnp.where(group_of == 0, mixed[:, :HD], 0.0)
        for g in range(1, KVH):
            picked = jnp.where(group_of == g, mixed[:, g * HD : (g + 1) * HD], picked)
        attended[r] = picked

    residual_load.wait()
    squares = jnp.zeros((row_count, HD), jnp.float32)
    widened = []
    for h in range(QH):
        cols = slice(h * HD, (h + 1) * HD)
        resid = (residual_in[:, cols].astype(jnp.float32) + attended[:, h, :]).astype(jnp.bfloat16)
        resid_halves[h // (QH // 2), :, (h % (QH // 2)) * HD : (h % (QH // 2) + 1) * HD] = resid
        wide = resid.astype(jnp.float32)
        widened.append(wide)
        squares += wide * wide
    scale = lax.rsqrt(jnp.sum(squares, axis=-1, keepdims=True) * (1.0 / width) + 1e-05)
    for h in range(QH):
        normed = (widened[h] * scale * norm_gain[:, h * HD : (h + 1) * HD]).astype(jnp.bfloat16)
        rows_in[h // (QH // 2), me, :, (h % (QH // 2)) * HD : (h % (QH // 2) + 1) * HD] = normed

    pl.semaphore_wait(barrier, EXPERTS - 1 + members)

    def block_copy(block, send_sem, recv_sem, device_id):
        return pltpu.make_async_remote_copy(
            src_ref=rows_in.at[side, block],
            dst_ref=rows_in.at[side, block],
            send_sem=send_sem,
            recv_sem=recv_sem,
            device_id=device_id,
            device_id_type=MESH,
        )

    def row_copy(i):
        return block_copy(
            me, row_send.at[i], row_recv.at[i], {"shard": teams[i] * members + member}
        )

    def pass_copy(i, j):
        return block_copy(
            teams[i] * members + member,
            pass_send.at[i * members + j],
            pass_recv.at[i * members + j],
            {"shard": team * members + after(j)},
        )

    def side_copy(i, j):
        return block_copy(
            teams[i] * members + before(j),
            side_send.at[i * members + j],
            side_recv.at[i * members + j],
            {"side": other},
        )

    def part_copy(i, j):
        return pltpu.make_async_remote_copy(
            src_ref=parts.at[teams[i] * members + after(j)],
            dst_ref=partial.at[i * members + j],
            send_sem=part_send.at[i * members + j],
            recv_sem=part_recv.at[i * members + j],
            device_id={"shard": team * members + after(j)},
            device_id_type=MESH,
        )

    def sum_copy(i):
        return pltpu.make_async_remote_copy(
            src_ref=summed.at[i],
            dst_ref=returned.at[i],
            send_sem=sum_send.at[i],
            recv_sem=sum_recv.at[i],
            device_id={"shard": teams[i] * members + member},
            device_id_type=MESH,
        )

    for i in range(1, EXPERTS):
        row_copy(i).start()
    others(lambda j: pass_copy(0, j).start())
    for i in range(1, EXPERTS):
        row_copy(i).wait_recv()
        others(lambda j: pass_copy(i, j).start())
        side_copy(i, 0).start()
    for i in range(EXPERTS):

        def swap(j):
            pass_copy(i, j).wait_recv()
            side_copy(i, j).start()

        others(swap)
    loads[2].wait()
    loads[3].wait()
    own = rows_in[side].reshape(n * row_count, half)
    own_cols = pl.ds(pl.multiple_of(side * half, half), half)
    gate_pre = jnp.dot(own, gate_w[own_cols, :], preferred_element_type=jnp.float32)
    up_pre = jnp.dot(own, up_w[own_cols, :], preferred_element_type=jnp.float32)
    for i in range(EXPERTS):
        if i:
            side_copy(i, 0).wait_recv()
        others(lambda j: side_copy(i, j).wait_recv())
    swapped = rows_in[other].reshape(n * row_count, half)
    other_cols = pl.ds(pl.multiple_of(other * half, half), half)
    gate_pre += jnp.dot(swapped, gate_w[other_cols, :], preferred_element_type=jnp.float32)
    up_pre += jnp.dot(swapped, up_w[other_cols, :], preferred_element_type=jnp.float32)
    hidden = (gate_pre / (1.0 + jnp.exp(-gate_pre)) * up_pre).astype(jnp.bfloat16)
    loads[4].wait()
    parts[...] = (
        jnp.dot(hidden, down_w[...], preferred_element_type=jnp.float32)
        .astype(jnp.bfloat16)
        .reshape(n, row_count, half)
    )

    order = list(range(1, EXPERTS)) + [0]
    for i in order:
        others(lambda j: part_copy(i, j).start())

    def team_sum(i):
        def add(j, total):
            part_copy(i, j).wait_recv()
            return total + partial[i * members + j].astype(jnp.float32)

        return lax.fori_loop(
            1, members, add, parts[teams[i] * members + member].astype(jnp.float32)
        )

    for i in range(1, EXPERTS):
        summed[i] = team_sum(i).astype(jnp.bfloat16)
        sum_copy(i).start()
    total = row_weights[0] * team_sum(0)
    for i in range(1, EXPERTS):
        sum_copy(i).wait_recv()
        total += row_weights[i] * returned[i].astype(jnp.float32)
    out[...] = (resid_halves[side].astype(jnp.float32) + total).astype(jnp.bfloat16)

    for i in range(EXPERTS):
        if i:
            row_copy(i).wait_send()
            side_copy(i, 0).wait_send()
            sum_copy(i).wait_send()

        def finish(j):
            pass_copy(i, j).wait_send()
            side_copy(i, j).wait_send()
            part_copy(i, j).wait_send()

        others(finish)


def body(
    queries,
    cache_keys,
    cache_values,
    lengths,
    residual_in,
    norm_gain,
    expert_ids,
    gate_values,
    w_gate,
    w_up,
    w_down,
):
    row_count, width = residual_in.shape
    n = lax.axis_size("shard")
    half = width // 2
    hidden = w_down.shape[0]
    vmem = pl.BlockSpec(memory_space=pltpu.VMEM)
    smem = pl.BlockSpec(memory_space=pltpu.SMEM)
    anywhere = pl.BlockSpec(memory_space=pl.ANY)
    dma = pltpu.SemaphoreType.DMA
    return pl.pallas_call(
        functools.partial(kernel, n),
        out_shape=jax.ShapeDtypeStruct((row_count, half), jnp.bfloat16),
        in_specs=[smem, anywhere, anywhere, anywhere, anywhere, vmem, vmem, vmem, anywhere, anywhere, anywhere],
        out_specs=vmem,
        scratch_shapes=[
            pltpu.VMEM(queries.shape, jnp.bfloat16),
            pltpu.VMEM(residual_in.shape, jnp.bfloat16),
            pltpu.VMEM(cache_keys.shape, jnp.bfloat16),
            pltpu.VMEM(cache_values.shape, jnp.bfloat16),
            pltpu.VMEM(w_gate.shape, jnp.bfloat16),
            pltpu.VMEM(w_up.shape, jnp.bfloat16),
            pltpu.VMEM((hidden, half), jnp.bfloat16),
            pltpu.VMEM((row_count, QH, HD), jnp.float32),
            pltpu.VMEM((row_count, QH, HD), jnp.float32),
            pltpu.VMEM((2, row_count, half), jnp.bfloat16),
            pltpu.VMEM((2, n, row_count, half), jnp.bfloat16),
            pltpu.VMEM((n, row_count, half), jnp.bfloat16),
            pltpu.VMEM((n, row_count, half), jnp.bfloat16),
            pltpu.VMEM((EXPERTS, row_count, half), jnp.bfloat16),
            pltpu.VMEM((EXPERTS, row_count, half), jnp.bfloat16),
            dma((7,)),
            dma((EXPERTS,)),
            dma((EXPERTS,)),
            dma((n,)),
            dma((n,)),
            dma((n,)),
            dma((n,)),
            dma((n,)),
            dma((n,)),
            dma((EXPERTS,)),
            dma((EXPERTS,)),
        ],
        compiler_params=pltpu.CompilerParams(
            collective_id=0, has_side_effects=True, vmem_limit_bytes=56 * 1024 * 1024
        ),
    )(
        lengths,
        queries,
        cache_keys,
        cache_values,
        residual_in,
        norm_gain.reshape(1, width),
        expert_ids.T,
        gate_values.T,
        w_gate,
        w_up,
        w_down,
    )


def solution(mesh):
    placed = (
        P(("grp", "shard"), None),
        P(("grp", "shard"), None, None),
        P(("grp", "shard"), None, None),
        P(("grp", "shard")),
        P(("grp", "shard"), None),
        P(),
        P(("grp", "shard"), None),
        P(("grp", "shard"), None),
        P(None, "shard"),
        P(None, "shard"),
        P("shard", None),
    )
    return jax.shard_map(
        body, mesh=mesh, in_specs=placed, out_specs=P(("grp", "shard"), "side"), check_vma=False
    )
```
